32 devices in a mesh: dp: 8 (over y, x, core), col: 4 (over z).
Axes of the slice: x: 2, y: 2, z: 4, core: 2. Of those that a mesh axis runs over, the one named last changes fastest.
Arguments:
- grad_out: bfloat16 [2048, 3584], P('dp', 'col'), may hold values from -6 to 6
- residual: bfloat16 [2048, 3584], P('dp', 'col'), may hold values from -6 to 6
- confounders: bfloat16 [2048, 512], P('dp'), may hold values from -6 to 6
- gram_factor: float32 [512, 512], replicated, as said below
- proj_weight: bfloat16 [3584, 3584], P('dp', 'col'), may hold values from -0.09375 to 0.09375
- doc_lengths: int32 [2048], P(('dp', 'col')), may hold values from 1 to 512, as said below
Outputs:
- token_grad: float32 [2048, 3584], P(('dp', 'col'))
- weight_grad: float32 [3584, 3584], P('dp', 'col')
The draws below stay inside these ranges and needn't reach their ends.
Inputs may be any that keep to these rules, and one draw needn't show every extreme that they name: `gram_factor`: lower triangular with a positive diagonal. `doc_lengths`: at least one document has 512 tokens.
All inputs are finite; a program needn't handle non-finite values.
Results may differ from the reference program's by a relative error of at most 0.0026.
Values may be sent and summed in bfloat16 or wider, within the bound.
A program may use at most 64 MiB of HBM per device.

```python
import jax
import jax.numpy as jnp
from jax import lax

D = 3584
OUT = 3584
K = 512
LEN_MAX = 512
DOCS = 2048


def draw_gram_factor(key, part):
    key_diag = jax.random.fold_in(key, 11)
    key_lower = jax.random.fold_in(key, 12)
    diag_vals = jax.random.uniform(key_diag, (K,), jnp.float32, 0.35, 0.7)
    lower_vals = jax.random.normal(key_lower, (K, K), jnp.float32) * (0.15 / K ** 0.5)
    row_ids = jnp.arange(K)[:, None]
    col_ids = jnp.arange(K)[None, :]
    strict = (row_ids > col_ids).astype(jnp.float32)
    ident = (row_ids == col_ids).astype(jnp.float32)
    factor = lower_vals * strict + ident * diag_vals[:, None]
    return factor * DOCS ** 0.5


def draw_doc_lengths(key, part):
    key_expo = jax.random.fold_in(key, 21)
    key_extra = jax.random.fold_in(key, 22)
    top_expo = LEN_MAX.bit_length() - 1
    expo = jax.random.randint(key_expo, (DOCS,), 0, top_expo)
    base_len = jnp.left_shift(jnp.ones((DOCS,), jnp.int32), expo.astype(jnp.int32))
    extra = jnp.remainder(jax.random.randint(key_extra, (DOCS,), 0, 1 << 30), base_len)
    lengths = jnp.minimum(base_len + extra, LEN_MAX)
    return jnp.where(jnp.arange(DOCS) == 0, LEN_MAX, lengths).astype(jnp.int32)


def strengthened(drawn, rng, source, target, shards_of, factor):
    def block_of(axis_at):
        return (jnp.arange(drawn.shape[axis_at]) // (drawn.shape[axis_at] // shards_of)).reshape((-1,) + (1,) * (drawn.ndim - 1 - axis_at))

    one_side = jax.random.permutation(rng, shards_of)[block_of(target)]
    far = (block_of(target) + shards_of // 2) % shards_of
    return jnp.where((block_of(source) == one_side) | (block_of(source) == far), factor * drawn, drawn)


def block_scale(stream_key, extent, cuts, smallest, top_value):
    gain, own = 1.0, jax.random.fold_in(stream_key, 6)
    for axis_at, shards_of in cuts:
        heights = jnp.exp(jax.random.uniform(jax.random.fold_in(own, axis_at), (shards_of,), jnp.float32, smallest / len(cuts), top_value / len(cuts)))
        gain = gain * jnp.repeat(heights, extent[axis_at] // shards_of).reshape([-1 if axis == axis_at else 1 for axis in range(len(extent))])
    return gain


def scatter_about(key, shape, scale, bound, cuts=(), kind=jnp.bfloat16):
    drawn = scale * jax.random.normal(key, shape, jnp.float32)
    if cuts:
        drawn = drawn * block_scale(key, shape, cuts, -0.22, 0.18)
    return jnp.clip(drawn, -bound, bound).astype(kind)


def noise_with(key, dims, scale, bound, cuts, heavy, kind=jnp.bfloat16):
    array = scale * jax.random.normal(key, dims, jnp.float32)
    if cuts:
        array = array * block_scale(key, dims, cuts, -0.22, 0.18)
    return jnp.clip(strengthened(array, jax.random.fold_in(key, 3), *heavy), -bound, bound).astype(kind)


def setup_inputs(seed: int = 0) -> dict:
    key_list = jax.random.split(jax.random.key(seed), 7)
    grad_out = noise_with(key_list[0], (DOCS, OUT), 1.0, 6.0, ((0, 8), (1, 4)), (0, 1, 8, 2.0))
    residual = scatter_about(key_list[1], (DOCS, D), 1.0, 6.0, ((0, 8), (1, 4)))
    confounders = scatter_about(key_list[2], (DOCS, K), 1.0, 6.0, ((0, 8),))
    gram_factor = draw_gram_factor(jax.random.fold_in(key_list[6], 71), 0)
    proj_weight = scatter_about(key_list[4], (OUT, D), D ** -0.5, 0.09375, ((0, 8), (1, 4)))
    doc_lengths = draw_doc_lengths(jax.random.fold_in(key_list[6], 71), 0)
    return dict(grad_out=grad_out, residual=residual, confounders=confounders, gram_factor=gram_factor, proj_weight=proj_weight, doc_lengths=doc_lengths)


def solve_gram(factor, rhs):
    inner = lax.linalg.triangular_solve(factor, rhs, left_side=True, lower=True)
    return lax.linalg.triangular_solve(factor, inner, left_side=True, lower=True, transpose_a=True)

def reference(grad_out, residual, confounders, gram_factor, proj_weight, doc_lengths):
    resid_grad = jnp.dot(grad_out.astype(jnp.float32), proj_weight.astype(jnp.float32), preferred_element_type=jnp.float32)
    resid_grad_b = resid_grad.astype(jnp.bfloat16)
    moments = jnp.dot(confounders.T.astype(jnp.float32), resid_grad_b.astype(jnp.float32), preferred_element_type=jnp.float32)
    coef = solve_gram(gram_factor, moments)
    coef_b = coef.astype(jnp.bfloat16)
    pooled_grad = resid_grad - jnp.dot(confounders.astype(jnp.float32), coef_b.astype(jnp.float32), preferred_element_type=jnp.float32)
    token_grad = pooled_grad / doc_lengths.astype(jnp.float32)[:, None]
    weight_grad = jnp.dot(grad_out.T.astype(jnp.float32), residual.astype(jnp.float32), preferred_element_type=jnp.float32) * DOCS ** (-0.5)
    return (token_grad, weight_grad)
```

```python
import functools

import jax
import jax.numpy as jnp
from jax import lax
from jax.experimental import pallas as pl
from jax.experimental.pallas import tpu as pltpu
from jax.sharding import PartitionSpec as P


def solve_gram(factor, rhs):
    inner = lax.linalg.triangular_solve(factor, rhs, left_side=True, lower=True)
    return lax.linalg.triangular_solve(factor, inner, left_side=True, lower=True, transpose_a=True)


def shards(grad_out, residual, confounders, gram_factor, proj_weight, doc_lengths):
    grad_full = lax.all_gather(grad_out, "col", axis=1, tiled=True)
    docs_total = grad_out.shape[0] * lax.axis_size("dp")
    norm_scale = docs_total ** (-0.5)
    grad_block = grad_full
    summed = lax.psum_scatter(
        lax.dot_general(
            grad_block, residual, (((0,), (0,)), ((), ())), preferred_element_type=jnp.float32
        ),
        "dp",
        scatter_dimension=0,
        tiled=True,
    )
    weight_grad = summed * norm_scale
    grad_block = grad_full
    dense_grad = jnp.dot(
        grad_block,
        lax.all_gather(proj_weight, "dp", axis=0, tiled=True),
        preferred_element_type=jnp.float32,
    )
    dense_b = dense_grad.astype(jnp.bfloat16)
    partial_value = lax.dot_general(
        confounders, dense_b, (((0,), (0,)), ((), ())), preferred_element_type=jnp.float32
    )
    moments = lax.psum(partial_value, "dp")
    coef_b = solve_gram(gram_factor, moments).astype(jnp.bfloat16)
    pooled = dense_grad - jnp.dot(confounders, coef_b, preferred_element_type=jnp.float32)
    doc_grad = lax.all_to_all(pooled, "col", split_axis=0, concat_axis=1, tiled=True)
    token_grad = doc_grad / doc_lengths.astype(jnp.float32)[:, None]
    return (token_grad, weight_grad)


F32, BF16 = jnp.float32, jnp.bfloat16
EXACT = lax.Precision.HIGHEST


def dot(a, b, da=1, db=0, precision=None):
    return lax.dot_general(
        a, b, (((da,), (db,)), ((), ())), preferred_element_type=F32, precision=precision
    )


def exact(a, b, da=1, db=0):
    return dot(a, b, da, db, EXACT)


def invert_factor(l_ref, inv_ref):
    k, base = l_ref.shape[0], 128
    r = lax.broadcasted_iota(jnp.int32, (base, base), 0)
    c = lax.broadcasted_iota(jnp.int32, (base, base), 1)
    diag = r == c
    inv_ref[...] = jnp.zeros_like(inv_ref)
    blocks = [l_ref[o : o + base, o : o + base] for o in range(0, k, base)]
    parts = [jnp.where(diag, 1.0 / jnp.where(diag, b, 1.0), 0.0) for b in blocks]
    size = 1
    while size < base:
        low = (r // (2 * size) == c // (2 * size)) & (r // size > c // size)
        inner = [exact(jnp.where(low, b, 0.0), x) for b, x in zip(blocks, parts)]
        parts = [x - exact(x, t) for x, t in zip(parts, inner)]
        size *= 2
    for at, x in enumerate(parts):
        o = at * base
        inv_ref[o : o + base, o : o + base] = x
    while size < k:
        for o in range(0, k, 2 * size):
            mid, end = o + size, o + 2 * size
            t = exact(l_ref[mid:end, o:mid], inv_ref[o:mid, o:mid])
            inv_ref[mid:end, o:mid] = -exact(inv_ref[mid:end, mid:end], t)
        size *= 2


def kernel(
    n, m, scale,
    gt_ref, res_ref, conf_ref, fac_ref, w_ref, len_ref,
    tok_ref, dw_ref,
    gf, wf, rf, gx, r32, rb, mt, msib, mpre, mrecv, inv, cf, pb, prow, own,
    g_s, g_r, w_s, w_r, r_s, r_r, x_s, x_r, a_s, a_r, m_s, m_r, c_s, c_r, p_s, p_r,
):
    dp, col = lax.axis_index("dp"), lax.axis_index("col")
    core, chip = dp % 2, dp // 2
    sib = dp + 1 - 2 * core
    chips = n // 2
    width, docs = gt_ref.shape
    units = w_ref.shape[0]
    share = docs // m
    rows = width // n

    def to_dp(src, dst, s, r, d):
        return pltpu.make_async_remote_copy(
            src, dst, s, r, device_id={"dp": d}, device_id_type=pl.DeviceIdType.MESH
        )

    def to_col(src, dst, s, r, d):
        return pltpu.make_async_remote_copy(
            src, dst, s, r, device_id={"col": d}, device_id_type=pl.DeviceIdType.MESH
        )

    def same_core(step):
        return lax.rem(chip + step, chips) * 2 + core

    def slot_of(t):
        back = lax.rem(t, chips)
        at = lax.rem(chip + chips - back, chips) * 2
        return at + lax.rem(core + t // chips, 2)

    def gather_start(ref, full, ss, rr):
        copies = [
            to_dp(ref, full.at[dp], ss.at[k], rr.at[k], same_core(k)) for k in range(1, chips)
        ]
        copies.append(to_dp(ref, full.at[dp], ss.at[chips], rr.at[chips], sib))
        for copy in copies:
            copy.start()
        full[dp] = ref[...]

    def gather_wait(full, ss, rr, t):
        at = full.at[slot_of(t)]
        to_dp(at, at, ss.at[t], rr.at[t], sib).wait_recv()

    def gather_pass(full, ss, rr, t):
        at = full.at[slot_of(t)]
        to_dp(at, at, ss.at[chips + t], rr.at[chips + t], sib).start()

    def gather_end(ref, full, ss, rr):
        for t in range(1, n):
            to_dp(ref, full.at[dp], ss.at[t], rr.at[t], sib).wait_send()

    barrier = pltpu.get_barrier_semaphore()
    for k in range(1, n):
        pl.semaphore_signal(
            barrier, inc=1, device_id={"dp": lax.rem(dp + k, n)}, device_id_type=pl.DeviceIdType.MESH
        )
    for k in range(1, m):
        pl.semaphore_signal(
            barrier, inc=1, device_id={"col": lax.rem(col + k, m)}, device_id_type=pl.DeviceIdType.MESH
        )
    pl.semaphore_wait(barrier, n + m - 2)

    mine = pl.ds(pl.multiple_of(col * width, width), width)
    g_copies = [
        to_col(gt_ref, gf.at[mine], g_s.at[k], g_r.at[k], lax.rem(col + k, m)) for k in range(1, m)
    ]
    for copy in g_copies:
        copy.start()
    gather_start(w_ref, wf, w_s, w_r)
    gf[mine, :] = gt_ref[...]

    invert_factor(fac_ref, inv)

    for copy in g_copies:
        copy.wait_recv()

    def add_units(t, first=False):
        at = slot_of(t)
        piece = gf[pl.ds(pl.multiple_of(at * units, units), units), :]
        part = dot(piece, wf[at], 0, 0)
        r32[...] = part if first else r32[...] + part

    add_units(0, True)

    @pl.loop(1, chips)
    def _(t):
        gather_wait(wf, w_s, w_r, t)
        gather_pass(wf, w_s, w_r, t)
        add_units(t)

    @pl.loop(chips, n)
    def _(t):
        gather_wait(wf, w_s, w_r, t)
        add_units(t)

    rb[...] = r32[...].astype(BF16)
    mt[...] = dot(rb[...], conf_ref[...], 0, 0)

    a_copies = []
    for q in range(chips):
        there = pl.ds(pl.multiple_of((2 * q + 1 - core) * rows, rows), rows)
        a_copies.append(to_dp(mt.at[there], msib.at[q], a_s.at[q], a_r.at[q], sib))
    for copy in a_copies:
        copy.start()
    for copy in a_copies:
        copy.wait_recv()
    for q in range(chips):
        here = pl.ds(pl.multiple_of((2 * q + core) * rows, rows), rows)
        mpre[q] = mt[here, :] + msib[q]
    m_copies = []
    for k in range(1, chips):
        q = lax.rem(chip + k, chips)
        m_copies.append(to_dp(mpre.at[q], mrecv.at[k], m_s.at[k], m_r.at[k], same_core(k)))
    for copy in m_copies:
        copy.start()

    gather_start(res_ref, rf, r_s, r_r)
    x_copies = []
    for k in range(1, n):
        d = lax.rem(dp + k, n)
        piece = gf.at[pl.ds(pl.multiple_of(d * units, units), units)]
        x_copies.append(to_dp(piece, gx.at[dp], x_s.at[k], x_r.at[k], d))
    for copy in x_copies:
        copy.start()
    gx[dp] = gf[pl.ds(pl.multiple_of(dp * units, units), units), :]

    for copy in m_copies:
        copy.wait_recv()
    total = mpre[chip]
    for k in range(1, chips):
        total = total + mrecv[k]
    coef = exact(exact(total, inv[...], 1, 1), inv[...])
    own[...] = coef.astype(BF16)
    gather_start(own, cf, c_s, c_r)

    @pl.loop(1, chips)
    def _(t):
        gather_wait(cf, c_s, c_r, t)
        gather_pass(cf, c_s, c_r, t)

    @pl.loop(chips, n)
    def _(t):
        gather_wait(cf, c_s, c_r, t)

    coef_all = cf[...].reshape(width, cf.shape[2])
    r32[...] = r32[...] - dot(conf_ref[...], coef_all, 1, 1)
    pb[...] = r32[...].astype(BF16)
    p_copies = []
    for k in range(1, m):
        c = lax.rem(col + k, m)
        piece = pb.at[pl.ds(pl.multiple_of(c * share, share), share)]
        p_copies.append(to_col(piece, prow.at[col], p_s.at[k], p_r.at[k], c))
    for copy in p_copies:
        copy.start()

    def add_docs(t, first=False):
        at = slot_of(t)
        part = dot(gx[at], rf[at]) * scale
        dw_ref[...] = part if first else dw_ref[...] + part

    @pl.loop(1, chips)
    def _(t):
        gather_wait(rf, r_s, r_r, t)
        gather_pass(rf, r_s, r_r, t)

    add_docs(0, True)
    for copy in x_copies:
        copy.wait_recv()

    @pl.loop(1, chips)
    def _(t):
        add_docs(t)

    @pl.loop(chips, n)
    def _(t):
        gather_wait(rf, r_s, r_r, t)
        add_docs(t)

    for copy in p_copies:
        copy.wait_recv()
    prow[col] = pb[pl.ds(pl.multiple_of(col * share, share), share), :]
    for c in range(m):
        tok_ref[:, c * width : (c + 1) * width] = prow[c].astype(F32) / len_ref[...]

    gather_end(w_ref, wf, w_s, w_r)
    gather_end(res_ref, rf, r_s, r_r)
    gather_end(own, cf, c_s, c_r)
    for copy in g_copies + a_copies + m_copies + x_copies + p_copies:
        copy.wait_send()


def fused(n, m, grad_out, residual, confounders, gram_factor, proj_weight, doc_lengths):
    docs, width = grad_out.shape
    units, k = proj_weight.shape[0], confounders.shape[1]
    share, rows, chips = docs // m, width // n, n // 2
    sem = pltpu.SemaphoreType.DMA
    vmem = pl.BlockSpec(memory_space=pltpu.VMEM)
    return pl.pallas_call(
        functools.partial(kernel, n, m, (docs * n) ** (-0.5)),
        out_shape=(
            jax.ShapeDtypeStruct((share, width * m), F32),
            jax.ShapeDtypeStruct((units, width), F32),
        ),
        in_specs=[vmem] * 6,
        out_specs=(vmem, vmem),
        scratch_shapes=[
            pltpu.VMEM((width * m, docs), BF16),
            pltpu.VMEM((n, units, width), BF16),
            pltpu.VMEM((n, docs, width), BF16),
            pltpu.VMEM((n, units, docs), BF16),
            pltpu.VMEM((docs, width), F32),
            pltpu.VMEM((docs, width), BF16),
            pltpu.VMEM((width, k), F32),
            pltpu.VMEM((chips, rows, k), F32),
            pltpu.VMEM((chips, rows, k), F32),
            pltpu.VMEM((chips, rows, k), F32),
            pltpu.VMEM((k, k), F32),
            pltpu.VMEM((n, rows, k), BF16),
            pltpu.VMEM((docs, width), BF16),
            pltpu.VMEM((m, share, width), BF16),
            pltpu.VMEM((rows, k), BF16),
        ]
        + [sem((m,))] * 2 + [sem((n,))] * 6 + [sem((chips,))] * 4 + [sem((n,))] * 2 + [sem((m,))] * 2,
        compiler_params=pltpu.CompilerParams(
            collective_id=0, has_side_effects=True, vmem_limit_bytes=56 * 2**20
        ),
    )(
        grad_out.T, residual, confounders, gram_factor, proj_weight,
        doc_lengths.astype(F32)[:, None],
    )


def fits(n, m, grad_out, residual, confounders, gram_factor, proj_weight, doc_lengths):
    docs, width = grad_out.shape
    units, k = proj_weight.shape[0], gram_factor.shape[0]
    whole = width % 128 == 0 and docs % (16 * m) == 0 and units % 16 == 0 and width % (16 * n) == 0
    return whole and n % 2 == 0 and k >= 128 and k & (k - 1) == 0 and units * n == width * m and n <= 8


def solution(mesh):
    placed = (P("dp", "col"), P("dp", "col"), P("dp", None), P(), P("dp", "col"), P(("dp", "col")))
    n, m = mesh.shape["dp"], mesh.shape["col"]

    def local(*args):
        return fused(n, m, *args) if fits(n, m, *args) else shards(*args)

    return jax.shard_map(
        local,
        mesh=mesh,
        in_specs=placed,
        out_specs=(P(("dp", "col"), None), P("dp", "col")),
        check_vma=False,
    )
```

```python
import functools

import jax
import jax.numpy as jnp
from jax import lax
from jax.experimental import pallas as pl
from jax.experimental.pallas import tpu as pltpu
from jax.sharding import PartitionSpec as P


def solve_gram(factor, rhs):
    inner = lax.linalg.triangular_solve(factor, rhs, left_side=True, lower=True)
    return lax.linalg.triangular_solve(factor, inner, left_side=True, lower=True, transpose_a=True)


def shards(grad_out, residual, confounders, gram_factor, proj_weight, doc_lengths):
    grad_full = lax.all_gather(grad_out, "col", axis=1, tiled=True)
    docs_total = grad_out.shape[0] * lax.axis_size("dp")
    norm_scale = docs_total ** (-0.5)
    grad_block = grad_full
    summed = lax.psum_scatter(
        lax.dot_general(
            grad_block, residual, (((0,), (0,)), ((), ())), preferred_element_type=jnp.float32
        ),
        "dp",
        scatter_dimension=0,
        tiled=True,
    )
    weight_grad = summed * norm_scale
    grad_block = grad_full
    dense_grad = jnp.dot(
        grad_block,
        lax.all_gather(proj_weight, "dp", axis=0, tiled=True),
        preferred_element_type=jnp.float32,
    )
    dense_b = dense_grad.astype(jnp.bfloat16)
    partial_value = lax.dot_general(
        confounders, dense_b, (((0,), (0,)), ((), ())), preferred_element_type=jnp.float32
    )
    moments = lax.psum(partial_value, "dp")
    coef_b = solve_gram(gram_factor, moments).astype(jnp.bfloat16)
    pooled = dense_grad - jnp.dot(confounders, coef_b, preferred_element_type=jnp.float32)
    doc_grad = lax.all_to_all(pooled, "col", split_axis=0, concat_axis=1, tiled=True)
    token_grad = doc_grad / doc_lengths.astype(jnp.float32)[:, None]
    return (token_grad, weight_grad)


F32, BF16 = jnp.float32, jnp.bfloat16
EXACT = lax.Precision.HIGHEST


def dot(a, b, da=1, db=0, precision=None):
    return lax.dot_general(
        a, b, (((da,), (db,)), ((), ())), preferred_element_type=F32, precision=precision
    )


def exact(a, b, da=1, db=0):
    return dot(a, b, da, db, EXACT)


def invert_factor(l_ref, inv_ref, between):
    k, base = l_ref.shape[0], 128
    r = lax.broadcasted_iota(jnp.int32, (base, base), 0)
    c = lax.broadcasted_iota(jnp.int32, (base, base), 1)
    diag = r == c
    inv_ref[...] = jnp.zeros_like(inv_ref)
    blocks = [l_ref[o : o + base, o : o + base] for o in range(0, k, base)]
    parts = [jnp.where(diag, 1.0 / jnp.where(diag, b, 1.0), 0.0) for b in blocks]
    size = 1
    while size < base:
        low = (r // (2 * size) == c // (2 * size)) & (r // size > c // size)
        inner = [exact(jnp.where(low, b, 0.0), x) for b, x in zip(blocks, parts)]
        parts = [x - exact(x, t) for x, t in zip(parts, inner)]
        size *= 2
    for at, x in enumerate(parts):
        o = at * base
        inv_ref[o : o + base, o : o + base] = x
    between()
    while size < k:
        for o in range(0, k, 2 * size):
            mid, end = o + size, o + 2 * size
            t = exact(l_ref[mid:end, o:mid], inv_ref[o:mid, o:mid])
            inv_ref[mid:end, o:mid] = -exact(inv_ref[mid:end, mid:end], t)
        size *= 2


def kernel(
    n, m,
    gt_ref, res_ref, conf_ref, fac_ref, w_ref,
    tok_ref, dw_ref,
    gf, wf, rf, gx, r32, rb, mt, msib, mpre, mrecv, inv, cf, pb, prow, own,
    g_s, g_r, h_s, h_r, w_s, w_r, r_s, r_r, x_s, x_r, a_s, a_r, m_s, m_r, c_s, c_r, p_s, p_r,
):
    dp, col = lax.axis_index("dp"), lax.axis_index("col")
    core, chip = dp % 2, dp // 2
    sib = dp + 1 - 2 * core
    chips = n // 2
    width, docs = gt_ref.shape
    units = w_ref.shape[0]
    share = docs // m
    rows = width // n

    def to_dp(src, dst, s, r, d):
        return pltpu.make_async_remote_copy(
            src, dst, s, r, device_id={"dp": d}, device_id_type=pl.DeviceIdType.MESH
        )

    def to_col(src, dst, s, r, d):
        return pltpu.make_async_remote_copy(
            src, dst, s, r, device_id={"col": d}, device_id_type=pl.DeviceIdType.MESH
        )

    def same_core(step):
        return lax.rem(chip + step, chips) * 2 + core

    def chip_at(bx, by):
        return lax.rem(chip // 2 + by, 2) * 2 + lax.rem(chip + bx, 2)

    def slot_of(t):
        at_core = lax.rem(core + t // chips, 2)
        one, two = lax.rem(t, 2), lax.rem(t, chips) // 2
        bx = (1 - at_core) * one + at_core * two
        by = at_core * one + (1 - at_core) * two
        return chip_at(bx, by) * 2 + at_core

    side_a, side_b = chip_at(1 - core, core) * 2 + core, chip_at(core, 1 - core) * 2 + core

    def gather_start(ref, full, ss, rr):
        for k, d in ((1, side_a), (2, side_b), (chips, sib)):
            to_dp(ref, full.at[dp], ss.at[k], rr.at[k], d).start()
        full[dp] = ref[...]

    def gather_wait(full, ss, rr, t):
        at = full.at[slot_of(t)]
        to_dp(at, at, ss.at[t], rr.at[t], sib).wait_recv()

    def gather_pass(full, ss, rr, t):
        at = full.at[slot_of(t)]
        if t == 1:
            to_dp(at, at, ss.at[3], rr.at[3], side_b).start()
        to_dp(at, at, ss.at[chips + t], rr.at[chips + t], sib).start()

    def gather_end(ref, full, ss, rr):
        for t in range(1, n):
            to_dp(ref, full.at[dp], ss.at[t], rr.at[t], sib).wait_send()

    barrier = pltpu.get_barrier_semaphore()
    for k in range(1, n):
        pl.semaphore_signal(
            barrier, inc=1, device_id={"dp": lax.rem(dp + k, n)}, device_id_type=pl.DeviceIdType.MESH
        )
    for k in range(1, m):
        pl.semaphore_signal(
            barrier, inc=1, device_id={"col": lax.rem(col + k, m)}, device_id_type=pl.DeviceIdType.MESH
        )
    pl.semaphore_wait(barrier, n + m - 2)

    def shard_at(c):
        return gf.at[pl.ds(pl.multiple_of(c * width, width), width)]

    def right(s):
        at = shard_at(lax.max(col - (s - 1), 0))
        return to_col(at, at, g_s.at[s], g_r.at[s], lax.rem(col + 1, m))

    def left(s):
        at = shard_at(lax.min(col + (s - 1), m - 1))
        return to_col(at, at, h_s.at[s], h_r.at[s], lax.rem(col + m - 1, m))

    def line_send(s, act):
        @pl.when((col >= s - 1) & (col + 1 < m))
        def _():
            act(right(s))

        @pl.when((col + s - 1 < m) & (col >= 1))
        def _():
            act(left(s))

    def line_wait(s):
        @pl.when(col >= s)
        def _():
            right(s).wait_recv()

        @pl.when(col + s < m)
        def _():
            left(s).wait_recv()

    gf[pl.ds(pl.multiple_of(col * width, width), width), :] = gt_ref[...]
    line_send(1, lambda copy: copy.start())
    gather_start(w_ref, wf, w_s, w_r)

    def line_next():
        line_wait(1)
        line_send(2, lambda copy: copy.start())

    invert_factor(fac_ref, inv, line_next)

    for t in (1, 2):
        gather_wait(wf, w_s, w_r, t)
        gather_pass(wf, w_s, w_r, t)
    for s in range(2, m - 1):
        line_wait(s)
        line_send(s + 1, lambda copy: copy.start())
    gather_wait(wf, w_s, w_r, 3)
    gather_pass(wf, w_s, w_r, 3)
    gather_start(res_ref, rf, r_s, r_r)
    line_wait(m - 1)

    def add_units(t, first=False):
        at = slot_of(t)
        piece = gf[pl.ds(pl.multiple_of(at * units, units), units), :]
        part = dot(piece, wf[at], 0, 0)
        r32[...] = part if first else r32[...] + part

    add_units(0, True)

    @pl.loop(1, chips)
    def _(t):
        add_units(t)

    @pl.loop(chips, n)
    def _(t):
        gather_wait(wf, w_s, w_r, t)
        add_units(t)

    rb[...] = r32[...].astype(BF16)
    mt[...] = dot(rb[...], conf_ref[...], 0, 0)

    a_copies = []
    for q in range(chips):
        there = pl.ds(pl.multiple_of((2 * q + 1 - core) * rows, rows), rows)
        a_copies.append(to_dp(mt.at[there], msib.at[q], a_s.at[q], a_r.at[q], sib))
    for copy in a_copies:
        copy.start()
    for copy in a_copies:
        copy.wait_recv()
    for q in range(chips):
        here = pl.ds(pl.multiple_of((2 * q + core) * rows, rows), rows)
        mpre[q] = mt[here, :] + msib[q]
    m_copies = []
    for k in range(1, chips):
        q = lax.rem(chip + k, chips)
        m_copies.append(to_dp(mpre.at[q], mrecv.at[k], m_s.at[k], m_r.at[k], same_core(k)))
    for copy in m_copies:
        copy.start()

    x_copies = []
    for k in range(1, n):
        d = lax.rem(dp + k, n)
        piece = gf.at[pl.ds(pl.multiple_of(d * units, units), units)]
        x_copies.append(to_dp(piece, gx.at[dp], x_s.at[k], x_r.at[k], d))
    for copy in x_copies:
        copy.start()
    gx[dp] = gf[pl.ds(pl.multiple_of(dp * units, units), units), :]

    for t in (1, 2):
        gather_wait(rf, r_s, r_r, t)
        gather_pass(rf, r_s, r_r, t)
    for copy in m_copies:
        copy.wait_recv()
    total = mpre[chip]
    for k in range(1, chips):
        total = total + mrecv[k]
    coef = exact(exact(total, inv[...], 1, 1), inv[...])
    own[...] = coef.astype(BF16)
    gather_start(own, cf, c_s, c_r)

    for t in range(1, chips):
        gather_wait(cf, c_s, c_r, t)
        gather_pass(cf, c_s, c_r, t)

    @pl.loop(chips, n)
    def _(t):
        gather_wait(cf, c_s, c_r, t)

    coef_all = cf[...].reshape(width, cf.shape[2])
    r32[...] = r32[...] - dot(conf_ref[...], coef_all, 1, 1)
    pb[...] = r32[...].astype(BF16)
    p_copies = []
    for k in range(1, m):
        c = lax.rem(col + k, m)
        piece = pb.at[pl.ds(pl.multiple_of(c * share, share), share)]
        p_copies.append(to_col(piece, prow.at[col], p_s.at[k], p_r.at[k], c))
    for copy in p_copies:
        copy.start()

    def add_docs(t, first=False):
        at = slot_of(t)
        part = dot(gx[at], rf[at])
        dw_ref[...] = part if first else dw_ref[...] + part

    gather_wait(rf, r_s, r_r, 3)
    gather_pass(rf, r_s, r_r, 3)

    add_docs(0, True)
    for copy in x_copies:
        copy.wait_recv()

    @pl.loop(1, chips)
    def _(t):
        add_docs(t)

    @pl.loop(chips, n)
    def _(t):
        gather_wait(rf, r_s, r_r, t)
        add_docs(t)

    for copy in p_copies:
        copy.wait_recv()
    prow[col] = pb[pl.ds(pl.multiple_of(col * share, share), share), :]
    for c in range(m):
        tok_ref[:, c * width : (c + 1) * width] = prow[c]

    gather_end(w_ref, wf, w_s, w_r)
    gather_end(res_ref, rf, r_s, r_r)
    gather_end(own, cf, c_s, c_r)
    for s in range(1, m):
        line_send(s, lambda copy: copy.wait_send())
    for copy in a_copies + m_copies + x_copies + p_copies:
        copy.wait_send()


def fused(n, m, grad_out, residual, confounders, gram_factor, proj_weight, doc_lengths):
    docs, width = grad_out.shape
    units, k = proj_weight.shape[0], confounders.shape[1]
    share, rows, chips = docs // m, width // n, n // 2
    sem = pltpu.SemaphoreType.DMA
    vmem = pl.BlockSpec(memory_space=pltpu.VMEM)
    rows_out, total = pl.pallas_call(
        functools.partial(kernel, n, m),
        out_shape=(
            jax.ShapeDtypeStruct((share, width * m), BF16),
            jax.ShapeDtypeStruct((units, width), F32),
        ),
        in_specs=[vmem] * 5,
        out_specs=(vmem, vmem),
        scratch_shapes=[
            pltpu.VMEM((width * m, docs), BF16),
            pltpu.VMEM((n, units, width), BF16),
            pltpu.VMEM((n, docs, width), BF16),
            pltpu.VMEM((n, units, docs), BF16),
            pltpu.VMEM((docs, width), F32),
            pltpu.VMEM((docs, width), BF16),
            pltpu.VMEM((width, k), F32),
            pltpu.VMEM((chips, rows, k), F32),
            pltpu.VMEM((chips, rows, k), F32),
            pltpu.VMEM((chips, rows, k), F32),
            pltpu.VMEM((k, k), F32),
            pltpu.VMEM((n, rows, k), BF16),
            pltpu.VMEM((docs, width), BF16),
            pltpu.VMEM((m, share, width), BF16),
            pltpu.VMEM((rows, k), BF16),
        ]
        + [sem((m,))] * 4 + [sem((n,))] * 6 + [sem((chips,))] * 4 + [sem((n,))] * 2 + [sem((m,))] * 2,
        compiler_params=pltpu.CompilerParams(
            collective_id=0, has_side_effects=True, vmem_limit_bytes=56 * 2**20
        ),
    )(grad_out.T, residual, confounders, gram_factor, proj_weight)
    return rows_out.astype(F32) / doc_lengths.astype(F32)[:, None], total * (docs * n) ** (-0.5)


def fits(n, m, grad_out, residual, confounders, gram_factor, proj_weight, doc_lengths):
    docs, width = grad_out.shape
    units, k = proj_weight.shape[0], gram_factor.shape[0]
    whole = width % 128 == 0 and docs % (16 * m) == 0 and units % 16 == 0 and width % (16 * n) == 0
    return whole and n == 8 and m > 2 and k >= 128 and k & (k - 1) == 0 and units * n == width * m


def solution(mesh):
    placed = (P("dp", "col"), P("dp", "col"), P("dp", None), P(), P("dp", "col"), P(("dp", "col")))
    n, m = mesh.shape["dp"], mesh.shape["col"]

    def local(*args):
        return fused(n, m, *args) if fits(n, m, *args) else shards(*args)

    return jax.shard_map(
        local,
        mesh=mesh,
        in_specs=placed,
        out_specs=(P(("dp", "col"), None), P("dp", "col")),
        check_vma=False,
    )
```

```python
import functools

import jax
import jax.numpy as jnp
from jax import lax
from jax.experimental import pallas as pl
from jax.experimental.pallas import tpu as pltpu
from jax.sharding import PartitionSpec as P


def solve_gram(factor, rhs):
    inner = lax.linalg.triangular_solve(factor, rhs, left_side=True, lower=True)
    return lax.linalg.triangular_solve(factor, inner, left_side=True, lower=True, transpose_a=True)


def shards(grad_out, residual, confounders, gram_factor, proj_weight, doc_lengths):
    grad_full = lax.all_gather(grad_out, "col", axis=1, tiled=True)
    docs_total = grad_out.shape[0] * lax.axis_size("dp")
    norm_scale = docs_total ** (-0.5)
    grad_block = grad_full
    summed = lax.psum_scatter(
        lax.dot_general(
            grad_block, residual, (((0,), (0,)), ((), ())), preferred_element_type=jnp.float32
        ),
        "dp",
        scatter_dimension=0,
        tiled=True,
    )
    weight_grad = summed * norm_scale
    grad_block = grad_full
    dense_grad = jnp.dot(
        grad_block,
        lax.all_gather(proj_weight, "dp", axis=0, tiled=True),
        preferred_element_type=jnp.float32,
    )
    dense_b = dense_grad.astype(jnp.bfloat16)
    partial_value = lax.dot_general(
        confounders, dense_b, (((0,), (0,)), ((), ())), preferred_element_type=jnp.float32
    )
    moments = lax.psum(partial_value, "dp")
    coef_b = solve_gram(gram_factor, moments).astype(jnp.bfloat16)
    pooled = dense_grad - jnp.dot(confounders, coef_b, preferred_element_type=jnp.float32)
    doc_grad = lax.all_to_all(pooled, "col", split_axis=0, concat_axis=1, tiled=True)
    token_grad = doc_grad / doc_lengths.astype(jnp.float32)[:, None]
    return (token_grad, weight_grad)


F32, BF16 = jnp.float32, jnp.bfloat16
EXACT = lax.Precision.HIGHEST


def dot(a, b, da=1, db=0, precision=None):
    return lax.dot_general(
        a, b, (((da,), (db,)), ((), ())), preferred_element_type=F32, precision=precision
    )


def exact(a, b, da=1, db=0):
    return dot(a, b, da, db, EXACT)


def invert_factor(l_ref, inv_ref, between):
    k, base = l_ref.shape[0], 128
    r = lax.broadcasted_iota(jnp.int32, (base, base), 0)
    c = lax.broadcasted_iota(jnp.int32, (base, base), 1)
    diag = r == c
    inv_ref[...] = jnp.zeros_like(inv_ref)
    blocks = [l_ref[o : o + base, o : o + base] for o in range(0, k, base)]
    parts = [jnp.where(diag, 1.0 / jnp.where(diag, b, 1.0), 0.0) for b in blocks]
    size = 1
    while size < base:
        low = (r // (2 * size) == c // (2 * size)) & (r // size > c // size)
        inner = [exact(jnp.where(low, b, 0.0), x) for b, x in zip(blocks, parts)]
        parts = [x - exact(x, t) for x, t in zip(parts, inner)]
        size *= 2
    for at, x in enumerate(parts):
        o = at * base
        inv_ref[o : o + base, o : o + base] = x
    between()
    while size < k:
        for o in range(0, k, 2 * size):
            mid, end = o + size, o + 2 * size
            t = exact(l_ref[mid:end, o:mid], inv_ref[o:mid, o:mid])
            inv_ref[mid:end, o:mid] = -exact(inv_ref[mid:end, mid:end], t)
        size *= 2


def kernel(
    n, m,
    gt_ref, res_ref, conf_ref, fac_ref, w_ref,
    tok_ref, dw_ref,
    gf, wf, rf, gx, r32, rb, mt, msib, mpre, mrecv, inv, cf, pb, prow, own,
    g_s, g_r, h_s, h_r, w_s, w_r, r_s, r_r, x_s, x_r, a_s, a_r, m_s, m_r, c_s, c_r, p_s, p_r,
):
    dp, col = lax.axis_index("dp"), lax.axis_index("col")
    core, chip = dp % 2, dp // 2
    sib = dp + 1 - 2 * core
    chips = n // 2
    width, docs = gt_ref.shape
    units = w_ref.shape[0]
    share = docs // m
    rows = width // n

    def to_dp(src, dst, s, r, d):
        return pltpu.make_async_remote_copy(
            src, dst, s, r, device_id={"dp": d}, device_id_type=pl.DeviceIdType.MESH
        )

    def to_col(src, dst, s, r, d):
        return pltpu.make_async_remote_copy(
            src, dst, s, r, device_id={"col": d}, device_id_type=pl.DeviceIdType.MESH
        )

    def same_core(step):
        return lax.rem(chip + step, chips) * 2 + core

    def chip_at(bx, by):
        return lax.rem(chip // 2 + by, 2) * 2 + lax.rem(chip + bx, 2)

    def slot_of(t):
        at_core = lax.rem(core + t // chips, 2)
        one, two = lax.rem(t, 2), lax.rem(t, chips) // 2
        bx = (1 - at_core) * one + at_core * two
        by = at_core * one + (1 - at_core) * two
        return chip_at(bx, by) * 2 + at_core

    side_a, side_b = chip_at(1 - core, core) * 2 + core, chip_at(core, 1 - core) * 2 + core

    def gather_start(ref, full, ss, rr):
        for k, d in ((1, side_a), (2, side_b), (chips, sib)):
            to_dp(ref, full.at[dp], ss.at[k], rr.at[k], d).start()
        full[dp] = ref[...]

    def gather_wait(full, ss, rr, t):
        at = full.at[slot_of(t)]
        to_dp(at, at, ss.at[t], rr.at[t], sib).wait_recv()

    def gather_pass(full, ss, rr, t):
        at = full.at[slot_of(t)]
        if t == 1:
            to_dp(at, at, ss.at[3], rr.at[3], side_b).start()
        to_dp(at, at, ss.at[chips + t], rr.at[chips + t], sib).start()

    def gather_end(ref, full, ss, rr):
        for t in range(1, n):
            to_dp(ref, full.at[dp], ss.at[t], rr.at[t], sib).wait_send()

    barrier = pltpu.get_barrier_semaphore()
    for k in range(1, n):
        pl.semaphore_signal(
            barrier, inc=1, device_id={"dp": lax.rem(dp + k, n)}, device_id_type=pl.DeviceIdType.MESH
        )
    for k in range(1, m):
        pl.semaphore_signal(
            barrier, inc=1, device_id={"col": lax.rem(col + k, m)}, device_id_type=pl.DeviceIdType.MESH
        )
    pl.semaphore_wait(barrier, n + m - 2)

    def shard_at(c):
        return gf.at[pl.ds(pl.multiple_of(c * width, width), width)]

    def right(s):
        at = shard_at(lax.max(col - (s - 1), 0))
        return to_col(at, at, g_s.at[s], g_r.at[s], lax.rem(col + 1, m))

    def left(s):
        at = shard_at(lax.min(col + (s - 1), m - 1))
        return to_col(at, at, h_s.at[s], h_r.at[s], lax.rem(col + m - 1, m))

    def line_send(s, act):
        @pl.when((col >= s - 1) & (col + 1 < m))
        def _():
            act(right(s))

        @pl.when((col + s - 1 < m) & (col >= 1))
        def _():
            act(left(s))

    def line_wait(s):
        @pl.when(col >= s)
        def _():
            right(s).wait_recv()

        @pl.when(col + s < m)
        def _():
            left(s).wait_recv()

    gf[pl.ds(pl.multiple_of(col * width, width), width), :] = gt_ref[...]
    line_send(1, lambda copy: copy.start())
    gather_start(w_ref, wf, w_s, w_r)

    def line_next():
        line_wait(1)
        line_send(2, lambda copy: copy.start())

    invert_factor(fac_ref, inv, line_next)

    for t in (1, 2):
        gather_wait(wf, w_s, w_r, t)
        gather_pass(wf, w_s, w_r, t)
    for s in range(2, m - 1):
        line_wait(s)
        line_send(s + 1, lambda copy: copy.start())
    gather_wait(wf, w_s, w_r, 3)
    gather_pass(wf, w_s, w_r, 3)
    gather_start(res_ref, rf, r_s, r_r)
    line_wait(m - 1)

    def add_units(t, first=False):
        at = slot_of(t)
        piece = gf[pl.ds(pl.multiple_of(at * units, units), units), :]
        part = dot(piece, wf[at], 0, 0)
        r32[...] = part if first else r32[...] + part

    add_units(0, True)

    @pl.loop(1, chips)
    def _(t):
        add_units(t)

    @pl.loop(chips, n)
    def _(t):
        gather_wait(wf, w_s, w_r, t)
        add_units(t)

    rb[...] = r32[...].astype(BF16)
    mt[...] = dot(rb[...], conf_ref[...], 0, 0)

    a_copies = []
    for q in range(chips):
        there = pl.ds(pl.multiple_of((2 * q + 1 - core) * rows, rows), rows)
        a_copies.append(to_dp(mt.at[there], msib.at[q], a_s.at[q], a_r.at[q], sib))
    for copy in a_copies:
        copy.start()
    for copy in a_copies:
        copy.wait_recv()
    for q in range(chips):
        here = pl.ds(pl.multiple_of((2 * q + core) * rows, rows), rows)
        mpre[q] = mt[here, :] + msib[q]
    m_copies = []
    for k in range(1, chips):
        q = lax.rem(chip + k, chips)
        m_copies.append(to_dp(mpre.at[q], mrecv.at[k], m_s.at[k], m_r.at[k], same_core(k)))
    for copy in m_copies:
        copy.start()

    for t in (1, 2):
        gather_wait(rf, r_s, r_r, t)
        gather_pass(rf, r_s, r_r, t)
    for copy in m_copies:
        copy.wait_recv()
    total = mpre[chip]
    for k in range(1, chips):
        total = total + mrecv[k]
    coef = exact(exact(total, inv[...], 1, 1), inv[...])
    own[...] = coef.astype(BF16)
    gather_start(own, cf, c_s, c_r)
    x_copies = []
    for k in range(1, n):
        d = lax.rem(dp + k, n)
        piece = gf.at[pl.ds(pl.multiple_of(d * units, units), units)]
        x_copies.append(to_dp(piece, gx.at[dp], x_s.at[k], x_r.at[k], d))
    for copy in x_copies:
        copy.start()
    gx[dp] = gf[pl.ds(pl.multiple_of(dp * units, units), units), :]


    for t in range(1, chips):
        gather_wait(cf, c_s, c_r, t)
        gather_pass(cf, c_s, c_r, t)

    @pl.loop(chips, n)
    def _(t):
        gather_wait(cf, c_s, c_r, t)

    coef_all = cf[...].reshape(width, cf.shape[2])
    r32[...] = r32[...] - dot(conf_ref[...], coef_all, 1, 1)
    pb[...] = r32[...].astype(BF16)
    p_copies = []
    for k in range(1, m):
        c = lax.rem(col + k, m)
        piece = pb.at[pl.ds(pl.multiple_of(c * share, share), share)]
        p_copies.append(to_col(piece, prow.at[col], p_s.at[k], p_r.at[k], c))
    for copy in p_copies:
        copy.start()

    def add_docs(t, first=False):
        at = slot_of(t)
        if not first:
            k = lax.rem(dp + n - at, n)
            to_dp(gx.at[at], gx.at[at], x_s.at[k], x_r.at[k], sib).wait_recv()
        part = dot(gx[at], rf[at])
        dw_ref[...] = part if first else dw_ref[...] + part

    gather_wait(rf, r_s, r_r, 3)
    gather_pass(rf, r_s, r_r, 3)

    add_docs(0, True)

    @pl.loop(1, chips)
    def _(t):
        add_docs(t)

    @pl.loop(chips, n)
    def _(t):
        gather_wait(rf, r_s, r_r, t)
        add_docs(t)

    for copy in p_copies:
        copy.wait_recv()
    prow[col] = pb[pl.ds(pl.multiple_of(col * share, share), share), :]
    for c in range(m):
        tok_ref[:, c * width : (c + 1) * width] = prow[c]

    gather_end(w_ref, wf, w_s, w_r)
    gather_end(res_ref, rf, r_s, r_r)
    gather_end(own, cf, c_s, c_r)
    for s in range(1, m):
        line_send(s, lambda copy: copy.wait_send())
    for copy in a_copies + m_copies + x_copies + p_copies:
        copy.wait_send()


def fused(n, m, grad_out, residual, confounders, gram_factor, proj_weight, doc_lengths):
    docs, width = grad_out.shape
    units, k = proj_weight.shape[0], confounders.shape[1]
    share, rows, chips = docs // m, width // n, n // 2
    sem = pltpu.SemaphoreType.DMA
    vmem = pl.BlockSpec(memory_space=pltpu.VMEM)
    rows_out, total = pl.pallas_call(
        functools.partial(kernel, n, m),
        out_shape=(
            jax.ShapeDtypeStruct((share, width * m), BF16),
            jax.ShapeDtypeStruct((units, width), F32),
        ),
        in_specs=[vmem] * 5,
        out_specs=(vmem, vmem),
        scratch_shapes=[
            pltpu.VMEM((width * m, docs), BF16),
            pltpu.VMEM((n, units, width), BF16),
            pltpu.VMEM((n, docs, width), BF16),
            pltpu.VMEM((n, units, docs), BF16),
            pltpu.VMEM((docs, width), F32),
            pltpu.VMEM((docs, width), BF16),
            pltpu.VMEM((width, k), F32),
            pltpu.VMEM((chips, rows, k), F32),
            pltpu.VMEM((chips, rows, k), F32),
            pltpu.VMEM((chips, rows, k), F32),
            pltpu.VMEM((k, k), F32),
            pltpu.VMEM((n, rows, k), BF16),
            pltpu.VMEM((docs, width), BF16),
            pltpu.VMEM((m, share, width), BF16),
            pltpu.VMEM((rows, k), BF16),
        ]
        + [sem((m,))] * 4 + [sem((n,))] * 6 + [sem((chips,))] * 4 + [sem((n,))] * 2 + [sem((m,))] * 2,
        compiler_params=pltpu.CompilerParams(
            collective_id=0, has_side_effects=True, vmem_limit_bytes=56 * 2**20
        ),
    )(grad_out.T, residual, confounders, gram_factor, proj_weight)
    return rows_out.astype(F32) / doc_lengths.astype(F32)[:, None], total * (docs * n) ** (-0.5)


def fits(n, m, grad_out, residual, confounders, gram_factor, proj_weight, doc_lengths):
    docs, width = grad_out.shape
    units, k = proj_weight.shape[0], gram_factor.shape[0]
    whole = width % 128 == 0 and docs % (16 * m) == 0 and units % 16 == 0 and width % (16 * n) == 0
    return whole and n == 8 and m > 2 and k >= 128 and k & (k - 1) == 0 and units * n == width * m


def solution(mesh):
    placed = (P("dp", "col"), P("dp", "col"), P("dp", None), P(), P("dp", "col"), P(("dp", "col")))
    n, m = mesh.shape["dp"], mesh.shape["col"]

    def local(*args):
        return fused(n, m, *args) if fits(n, m, *args) else shards(*args)

    return jax.shard_map(
        local,
        mesh=mesh,
        in_specs=placed,
        out_specs=(P(("dp", "col"), None), P("dp", "col")),
        check_vma=False,
    )
```
